32 devices in a mesh: parts: 2 (over y), expert: 4 (over z), hidden: 2 (over x), rep: 2 (over core).
Axes of the slice: x: 2, y: 2, z: 4, core: 2. Of those that a mesh axis runs over, the one named last changes fastest.
Arguments:
- tokens: bfloat16 [1024, 4096], P(('parts', 'expert', 'rep'), 'hidden'), parts along dimension 0, may hold values from -6 to 6
- route_ids: int32 [1024, 2], P(('parts', 'expert', 'rep')), parts along dimension 0, may hold values from 0 to 3, all different within a row; in each aligned block of 64 rows (0 to 63, 64 to 127, ...) at most 48 rows name the same one
- route_weight: float32 [1024, 2], P(('parts', 'expert', 'rep')), parts along dimension 0, may hold values from 0.1 to 1
- user_slot: int32 [128, 4], P(('parts', 'expert', 'rep')), parts along dimension 0, may hold values from 0 to 15
- gate_weight: bfloat16 [4, 4096, 1536], P('expert', None, 'hidden'), may hold values from -0.09375 to 0.09375
- up_weight: bfloat16 [4, 4096, 1536], P('expert', None, 'hidden'), may hold values from -0.09375 to 0.09375
- down_weight: bfloat16 [4, 1536, 4096], P('expert', 'hidden'), may hold values from -0.15625 to 0.15625
- adapter_down: bfloat16 [4, 4096, 128], P('expert', 'hidden'), may hold values from -0.09375 to 0.09375
- adapter_up: bfloat16 [4, 128, 1536], P('expert', None, 'hidden'), may hold values from -2 to 2
Outputs:
- mixed: bfloat16 [1024, 4096], P(('parts', 'expert', 'rep'), 'hidden'), parts along dimension 0
The draws below stay inside these ranges and needn't reach their ends.
There are 2 independent parts, one for each index of `parts`. The reference program is written for one: setup_inputs(seed, part) draws one part's arguments, and reference() takes and returns one part's arrays. A program takes and returns all parts, laid end to end along the dimension named above; an argument that names none is the same for every part. Nothing has to cross between parts.
Inputs may be any that keep to these rules, and one draw needn't show every extreme that they name: `route_ids`: each row names 2 different experts. Among the 64 rows of one device (aligned blocks), no expert is named by more than 48 rows, a bound that some block reaches.
All inputs are finite; a program needn't handle non-finite values.
Results may differ from the reference program's by a relative error of at most 0.015.
Values may be sent and summed in bfloat16 or wider, within the bound.
A program may use at most 64 MiB of HBM per device.

```python
import math
import jax
import jax.numpy as jnp
import numpy as np
from jax import lax

D = 4096
FF = 1536
RANK = 8
SLOTS = 16
USER_TOK = 8
TOK_DEV = 64
EXPERTS = 4
TOP = 2
CAP = 48
ADAPT = 128
TOKENS = 512
USERS = 64
N_HIDDEN = 2


def place_ends(drawn, key, low, top_value):
    longest = drawn.shape.index(max(drawn.shape))
    spots = []
    for shift in (0, 1):
        where = [jax.random.randint(jax.random.fold_in(key, axis), (), 0, length) for axis, length in enumerate(drawn.shape)]
        where[longest] = (where[longest] + shift) % drawn.shape[longest]
        spots.append(tuple(where))
    return drawn.at[spots[0]].set(low).at[spots[1]].set(top_value)


def block_levels(rng, dims, pieces, smallest, high):
    def one(dim, parts):
        steps = jax.random.uniform(jax.random.fold_in(jax.random.fold_in(rng, 6), dim), (parts,), jnp.float32, smallest / len(pieces), high / len(pieces))
        return jnp.repeat(jnp.exp(steps), dims[dim] // parts).reshape((-1,) + (1,) * (len(dims) - dim - 1))

    factor_of = one(*pieces[0])
    for cut in pieces[1:]:
        factor_of = factor_of * one(*cut)
    return factor_of


def deal_out(key, own, number, rows, count, top, most, lean):
    sequence = jax.random.permutation(key, count)
    heavy_load, common = shares(count, rows * top, most, lean, True), shares(count, rows * top, most, lean, False)
    places = jnp.arange(count)

    def named(lengths, rotation):
        used = int((lengths > 0).sum())
        fixed = max(1, used // 4)
        shifted = fixed + (places - fixed + rotation * (used - fixed)) % max(1, count - fixed)
        return jnp.zeros((count,), jnp.int32).at[sequence[jnp.where(places < fixed, places, shifted)]].set(jnp.asarray(lengths, jnp.int32))

    lengths = jnp.where(number % 4 == 0, named(heavy_load, number // 4), named(common, number - number // 4 - 1))
    mixed = jax.random.permutation(jax.random.fold_in(own, 3), count)
    donor, sink = mixed[0:count // 2 * 2:2], mixed[1:count // 2 * 2:2]
    slack = jnp.minimum(lengths[donor] - 1, most - lengths[sink]) // 2
    slack = jnp.where((donor == sequence[0]) | (sink == sequence[0]) | (lengths[sink] == 0), 0, jnp.maximum(slack, 0))
    shifted = jax.random.randint(jax.random.fold_in(own, 4), (count // 2,), 0, 1 << 20) % (slack + 1)
    lengths = lengths.at[donor].add(-shifted).at[sink].add(shifted)
    labels = jnp.searchsorted(jnp.cumsum(lengths), jnp.arange(rows * top), side="right").astype(jnp.int32)
    table = labels.reshape(top, rows).T
    table = table[jax.random.permutation(jax.random.fold_in(own, 1), rows)]
    rotation = jax.random.randint(jax.random.fold_in(own, 2), (rows, 1), 0, top)
    return jnp.take_along_axis(table, (jnp.arange(top)[None, :] + rotation) % top, axis=1)


def shares(number_of, total, bound, lean, full):
    weights = [(1 << 20) // math.isqrt(standing ** lean) + 1 for standing in range(1, number_of + 1)]
    largest = bound if full else min(bound, max(-(-total // number_of), total * weights[0] // sum(weights)))
    least = 1 if total - largest >= number_of - 1 else 0
    holding, rest = [largest] + [least] * (number_of - 1), total - largest - least * (number_of - 1)
    while rest > 0:
        candidates = [i for i in range(1, number_of) if holding[i] < largest] or [i for i in range(1, number_of) if holding[i] < bound]
        whole, left = sum([weights[i] for i in candidates]), rest
        for i in candidates:
            addition = min(bound - holding[i], max(1, left * weights[i] // whole), rest)
            holding[i] = holding[i] + addition
            rest = rest - addition
    return np.array(holding)


def gaussian(stream_key, shape, scale, bound, shards=(), dtype=jnp.bfloat16):
    level = block_levels(stream_key, shape, shards, -0.22, 0.18) if shards else 1.0
    entries = jax.random.normal(stream_key, shape, jnp.float32) * scale * level
    return jnp.minimum(jnp.maximum(entries, -bound), bound).astype(dtype)


def setup_inputs(seed: int = 0, part: int = 0) -> dict:
    key_list = jax.random.split(jax.random.key(seed), 10)
    own_keys = jax.random.split(jax.random.fold_in(key_list[9], part), 10)
    tokens = gaussian(own_keys[0], (TOKENS, D), 1.0, 6.0, ((0, 8), (1, 2)))
    route_ids_keys = jax.random.split(jax.random.fold_in(own_keys[1], 1), TOKENS // TOK_DEV)
    route_ids_turns = jax.random.permutation(jax.random.fold_in(own_keys[1], 3), TOKENS // TOK_DEV)
    route_ids = jax.vmap(lambda own, number: deal_out(jax.random.fold_in(own_keys[1], 2), own, number, TOK_DEV, EXPERTS, TOP, CAP, 2))(route_ids_keys, route_ids_turns).reshape((TOKENS, TOP))
    route_weight = jnp.clip(0.1 + 0.9 * jax.random.uniform(own_keys[2], (TOKENS, TOP), jnp.float32) ** block_levels(own_keys[2], (TOKENS, TOP), ((0, 8),), -0.2, 0.2), 0.1, 1.0)
    user_slot = place_ends(jax.random.randint(own_keys[3], (USERS, EXPERTS), 0, SLOTS), jax.random.fold_in(own_keys[3], 1), 0, SLOTS - 1).astype(jnp.int32)
    gate_weight = gaussian(key_list[4], (EXPERTS, D, FF), D ** -0.5, 0.09375, ((0, 4), (2, 2)))
    up_weight = gaussian(key_list[5], (EXPERTS, D, FF), D ** -0.5, 0.09375, ((0, 4), (2, 2)))
    down_weight = gaussian(key_list[6], (EXPERTS, FF, D), FF ** -0.5, 0.15625, ((0, 4), (1, 2)))
    adapter_down = gaussian(key_list[7], (EXPERTS, D, ADAPT), D ** -0.5, 0.09375, ((0, 4), (1, 2)))
    adapter_up = gaussian(key_list[8], (EXPERTS, ADAPT, FF), RANK ** -0.5, 2.0, ((0, 4), (2, 2)))
    return {"tokens": tokens, "route_ids": route_ids, "route_weight": route_weight, "user_slot": user_slot, "gate_weight": gate_weight, "up_weight": up_weight, "down_weight": down_weight, "adapter_down": adapter_down, "adapter_up": adapter_up}


def reference(tokens, route_ids, route_weight, user_slot, gate_weight, up_weight, down_weight, adapter_down, adapter_up):
    tokens_count = tokens.shape[0]
    user_of = (jnp.arange(tokens_count) // USER_TOK).astype(jnp.int32)
    slot_table = user_slot[user_of]
    row_positions = jnp.arange(tokens_count)
    group_width = FF // N_HIDDEN

    def per_expert(running, expert_number):
        gate_values = jnp.dot(tokens, gate_weight[expert_number], preferred_element_type=jnp.float32)
        up_values = jnp.dot(tokens, up_weight[expert_number], preferred_element_type=jnp.float32)
        chosen = slot_table[:, expert_number]
        rank_full = jnp.dot(tokens, adapter_down[expert_number], preferred_element_type=jnp.float32)
        rank_portion = rank_full.reshape(tokens_count, SLOTS, RANK)[row_positions, chosen].astype(jnp.bfloat16)
        upward_factor = adapter_up[expert_number].reshape(SLOTS, RANK, FF)[chosen]
        adapter_update = jnp.einsum("xl,xla->xa", rank_portion.astype(jnp.float32), upward_factor.astype(jnp.float32))
        hidden_act = (jax.nn.silu(gate_values) * (up_values + adapter_update)).astype(jnp.bfloat16)
        grouped = hidden_act.reshape(tokens_count, N_HIDDEN, group_width).astype(jnp.float32)
        down_groups = down_weight[expert_number].reshape(N_HIDDEN, group_width, D).astype(jnp.float32)
        partial_value = jnp.einsum("tgf,gfd->tgd", grouped, down_groups).astype(jnp.bfloat16)
        output = jnp.sum(partial_value.astype(jnp.float32), axis=1)
        weight = jnp.sum(jnp.where(route_ids == expert_number, route_weight, 0.0), axis=1)
        return running + weight[:, None] * output, None

    start = jnp.zeros((tokens_count, D), jnp.float32)
    total, _ = lax.scan(per_expert, start, jnp.arange(EXPERTS).astype(jnp.int32))
    return total.astype(jnp.bfloat16)
```

```python
import functools

import jax
import jax.numpy as jnp
from jax import lax
from jax.experimental import pallas as pl
from jax.experimental.pallas import tpu as pltpu
from jax.sharding import PartitionSpec as P

RANK = 8
MESH = pl.DeviceIdType.MESH
F32 = jnp.float32
BF16 = jnp.bfloat16


def tile_of(size, most):
    return most if size % most == 0 else size


def dot(a, b):
    return jnp.dot(a, b, preferred_element_type=F32)


def kernel(
    E,
    H,
    cap,
    tok_ref,
    ids_ref,
    wt_ref,
    slot_ref,
    gw_hbm,
    uw_hbm,
    dw_hbm,
    ad_hbm,
    au_hbm,
    out_ref,
    gw,
    uw,
    dw,
    ad,
    au,
    zsend,
    zrecv,
    xrows,
    xrank,
    rank_own,
    rank_out,
    act,
    pout,
    pin,
    yown,
    rbuf,
    ret,
    comb,
    w_sem,
    z_s,
    z_r,
    x_s,
    x_r,
    k_s,
    k_r,
    o_s,
    o_r,
    b_s,
    b_r,
):
    me_e = lax.axis_index("expert")
    me_h = lax.axis_index("hidden")
    T, Dsh = tok_ref.shape
    K = ids_ref.shape[0]
    U = slot_ref.shape[1]
    F = gw.shape[1]
    A = ad.shape[1]

    loads = [
        pltpu.make_async_copy(src.at[0], dst, w_sem.at[i])
        for i, (src, dst) in enumerate(
            ((ad_hbm, ad), (gw_hbm, gw), (uw_hbm, uw), (au_hbm, au), (dw_hbm, dw))
        )
    ]
    for load in loads:
        load.start()

    barrier = pltpu.get_barrier_semaphore()
    for d in range(1, E):
        pl.semaphore_signal(
            barrier, inc=1, device_id={"expert": lax.rem(me_e + d, E)}, device_id_type=MESH
        )
    for j in range(1, H):
        pl.semaphore_signal(
            barrier, inc=1, device_id={"hidden": lax.rem(me_h + j, H)}, device_id_type=MESH
        )

    def z_copy(d):
        return pltpu.make_async_remote_copy(
            src_ref=zsend.at[d],
            dst_ref=zrecv.at[d],
            send_sem=z_s.at[d],
            recv_sem=z_r.at[d],
            device_id={"expert": lax.rem(me_e + d, E)},
            device_id_type=MESH,
        )

    def x_copy(d, j):
        return pltpu.make_async_remote_copy(
            src_ref=zrecv.at[d, :, pl.ds(0, Dsh)],
            dst_ref=xrows.at[j, d],
            send_sem=x_s.at[j, d],
            recv_sem=x_r.at[j, d],
            device_id={"hidden": lax.rem(me_h + j, H)},
            device_id_type=MESH,
        )

    def k_copy(d, j):
        return pltpu.make_async_remote_copy(
            src_ref=rank_out.at[d],
            dst_ref=xrank.at[j, d],
            send_sem=k_s.at[j, d],
            recv_sem=k_r.at[j, d],
            device_id={"hidden": lax.rem(me_h + j, H)},
            device_id_type=MESH,
        )

    def o_copy(d, j):
        return pltpu.make_async_remote_copy(
            src_ref=pout.at[j, d],
            dst_ref=pin.at[j, d],
            send_sem=o_s.at[j, d],
            recv_sem=o_r.at[j, d],
            device_id={"hidden": lax.rem(me_h + j, H)},
            device_id_type=MESH,
        )

    def b_copy(d):
        return pltpu.make_async_remote_copy(
            src_ref=rbuf.at[d],
            dst_ref=ret.at[d],
            send_sem=b_s.at[d],
            recv_sem=b_r.at[d],
            device_id={"expert": lax.rem(me_e - d + E, E)},
            device_id_type=MESH,
        )

    R = max(E, 8)
    ids = ids_ref[...]
    wts = wt_ref[...]
    named = lax.rem(lax.broadcasted_iota(jnp.int32, (R, T), 0) + me_e, E)
    chosen = jnp.zeros((R, T), F32)
    weight = jnp.zeros((R, T), F32)
    for k in range(K):
        hit = ids[k : k + 1, :] == named
        chosen += jnp.where(hit, 1.0, 0.0)
        weight += jnp.where(hit, wts[k : k + 1, :], 0.0)
    before = lax.broadcasted_iota(jnp.int32, (T, T), 0) < lax.broadcasted_iota(
        jnp.int32, (T, T), 1
    )
    place = dot(chosen.astype(BF16), jnp.where(before, 1.0, 0.0).astype(BF16))
    place = jnp.where(chosen > 0.0, place, -1.0)
    row_no = lax.broadcasted_iota(jnp.int32, (cap, T), 0).astype(F32)
    picks = [row_no == place[d : d + 1, :] for d in range(E)]
    select = jnp.concatenate([jnp.where(p, 1.0, 0.0) for p in picks], axis=0).astype(BF16)
    slots = slot_ref[...].astype(F32)
    slot_no = lax.broadcasted_iota(jnp.int32, slots.shape, 0)
    eye = lax.broadcasted_iota(jnp.int32, (U, U), 0) == lax.broadcasted_iota(
        jnp.int32, (U, U), 1
    )
    column_slot = (lax.broadcasted_iota(jnp.int32, (U, A), 1) // RANK).astype(F32)

    def mask_of(d):
        row = jnp.sum(
            jnp.where(slot_no == lax.rem(me_e + d, E), slots, 0.0), axis=0, keepdims=True
        )
        column = jnp.sum(jnp.where(eye, row, 0.0), axis=1, keepdims=True)
        user = jnp.where(column == column_slot, 1.0, 0.0)
        tokens = jnp.broadcast_to(user[:, None, :], (U, T // U, A)).reshape(T, A)
        return dot(select[d * cap : (d + 1) * cap], tokens.astype(BF16)).astype(BF16)

    tok = tok_ref[...]
    picked = dot(select, tok).astype(BF16)
    for d in range(E):
        block = zrecv if d == 0 else zsend
        block[d, :, pl.ds(0, Dsh)] = picked[d * cap : (d + 1) * cap]
        block[d, :, pl.ds(Dsh, A)] = mask_of(d)

    pl.semaphore_wait(barrier, E + H - 2)
    for d in range(1, E):
        z_copy(d).start()

    loads[0].wait()

    def forward(d):
        for j in range(1, H):
            x_copy(d, j).start()
        mine = dot(zrecv[d, :, pl.ds(0, Dsh)], ad[...])
        mine = jnp.where(zrecv[d, :, pl.ds(Dsh, A)] > 0, mine, 0.0)
        rank_own[d] = mine
        rank_out[d] = mine.astype(BF16)
        for j in range(1, H):
            k_copy(d, j).start()

    forward(0)
    scaled = jnp.concatenate(
        [jnp.where(p, weight[d : d + 1, :], 0.0) for d, p in enumerate(picks)], axis=0
    ).T
    high = scaled.astype(BF16)
    comb[pl.ds(0, T), :] = high
    comb[pl.ds(T, T), :] = (scaled - high.astype(F32)).astype(BF16)
    for load in loads[1:]:
        load.wait()

    tf = tile_of(F, 256)
    tn = tile_of(Dsh, 512)

    def compute(d):
        for j in range(1, H):
            x_copy(d, j).wait_recv()
            k_copy(d, j).wait_recv()
        rank = rank_own[d]
        for j in range(1, H):
            rank += xrank[j, d].astype(F32)
        rank = rank.astype(BF16)

        for c in range(F // tf):
            columns = pl.ds(c * tf, tf)
            up = dot(rank, au[:, columns])
            gate = jnp.zeros_like(up)
            for j in range(H):
                rows = pl.ds(pl.multiple_of(lax.rem(me_h - j + H, H) * Dsh, Dsh), Dsh)
                left = zrecv[d, :, pl.ds(0, Dsh)] if j == 0 else xrows[j, d]
                gate += dot(left, gw[rows, columns])
                up += dot(left, uw[rows, columns])
            act[:, columns] = (gate / (1.0 + jnp.exp(-gate)) * up).astype(BF16)

        for j in list(range(1, H)) + [0]:
            start = lax.rem(me_h + j, H) * Dsh

            @pl.loop(0, Dsh // tn)
            def _(c):
                columns = pl.ds(pl.multiple_of(start + c * tn, tn), tn)
                part = dot(act[...], dw[:, columns]).astype(BF16)
                here = pl.ds(pl.multiple_of(c * tn, tn), tn)
                if j == 0:
                    yown[d, :, here] = part
                else:
                    pout[j, d, :, here] = part

            if j:
                o_copy(d, j).start()

    def give_back(d):
        total = yown[d].astype(F32)
        for j in range(1, H):
            o_copy(d, j).wait_recv()
            total += pin[j, d].astype(F32)
        rbuf[d] = total.astype(BF16)

        @pl.when(d > 0)
        def _():
            b_copy(d).start()

    @pl.loop(0, E)
    def _(d):
        @pl.when(d + 1 < E)
        def _():
            z_copy(d + 1).wait_recv()
            forward(d + 1)

        compute(d)

        @pl.when(d > 0)
        def _():
            give_back(d - 1)

    give_back(jnp.int32(E - 1))

    ret[0] = rbuf[0]
    for d in range(1, E):
        b_copy(d).wait_recv()
    both = dot(comb[...], ret[...].reshape(E * cap, Dsh))
    out_ref[...] = (both[:T] + both[T:]).astype(BF16)

    @pl.loop(0, E)
    def _(d):
        for j in range(1, H):
            x_copy(d, j).wait_send()
            k_copy(d, j).wait_send()
            o_copy(d, j).wait_send()

        @pl.when(d > 0)
        def _():
            z_copy(d).wait_send()
            b_copy(d).wait_send()


def local(
    tokens,
    route_ids,
    route_weight,
    user_slot,
    gate_weight,
    up_weight,
    down_weight,
    adapter_down,
    adapter_up,
):
    E = lax.axis_size("expert")
    H = lax.axis_size("hidden")
    T, K = route_ids.shape
    cap = T * K * 3 // (2 * E)
    Dsh = tokens.shape[1]
    D = gate_weight.shape[1]
    F = gate_weight.shape[2]
    A = adapter_down.shape[2]
    vmem = pl.BlockSpec(memory_space=pltpu.VMEM)
    hbm = pl.BlockSpec(memory_space=pl.ANY)
    dma = pltpu.SemaphoreType.DMA
    rows = E * cap
    flops = 2 * rows * (3 * D * F + Dsh * A + A * F)
    return pl.pallas_call(
        functools.partial(kernel, E, H, cap),
        out_shape=jax.ShapeDtypeStruct((T, Dsh), BF16),
        in_specs=[vmem] * 4 + [hbm] * 5,
        out_specs=vmem,
        scratch_shapes=[
            pltpu.VMEM((D, F), BF16),
            pltpu.VMEM((D, F), BF16),
            pltpu.VMEM((F, D), BF16),
            pltpu.VMEM((Dsh, A), BF16),
            pltpu.VMEM((A, F), BF16),
            pltpu.VMEM((E, cap, Dsh + A), BF16),
            pltpu.VMEM((E, cap, Dsh + A), BF16),
            pltpu.VMEM((H, E, cap, Dsh), BF16),
            pltpu.VMEM((H, E, cap, A), BF16),
            pltpu.VMEM((E, cap, A), F32),
            pltpu.VMEM((E, cap, A), BF16),
            pltpu.VMEM((cap, F), BF16),
            pltpu.VMEM((H, E, cap, Dsh), BF16),
            pltpu.VMEM((H, E, cap, Dsh), BF16),
            pltpu.VMEM((E, cap, Dsh), BF16),
            pltpu.VMEM((E, cap, Dsh), BF16),
            pltpu.VMEM((E, cap, Dsh), BF16),
            pltpu.VMEM((2 * T, rows), BF16),
            dma((5,)),
            dma((E,)),
            dma((E,)),
            dma((H, E)),
            dma((H, E)),
            dma((H, E)),
            dma((H, E)),
            dma((H, E)),
            dma((H, E)),
            dma((E,)),
            dma((E,)),
        ],
        compiler_params=pltpu.CompilerParams(
            collective_id=0, has_side_effects=True, vmem_limit_bytes=56 * 1024 * 1024
        ),
        cost_estimate=pl.CostEstimate(
            flops=flops, bytes_accessed=6 * D * F, transcendentals=rows * F
        ),
    )(
        tokens,
        route_ids.T,
        route_weight.T,
        user_slot.T,
        gate_weight,
        up_weight,
        down_weight,
        adapter_down,
        adapter_up,
    )


def solution(mesh):
    in_specs = (
        P(("parts", "expert", "rep"), "hidden"),
        P(("parts", "expert", "rep"), None),
        P(("parts", "expert", "rep"), None),
        P(("parts", "expert", "rep"), None),
        P("expert", None, "hidden"),
        P("expert", None, "hidden"),
        P("expert", "hidden", None),
        P("expert", "hidden", None),
        P("expert", None, "hidden"),
    )
    out_specs = P(("parts", "expert", "rep"), "hidden")
    return jax.shard_map(local, mesh=mesh, in_specs=in_specs, out_specs=out_specs, check_vma=False)
```

```python
import functools

import jax
import jax.numpy as jnp
from jax import lax
from jax.experimental import pallas as pl
from jax.experimental.pallas import tpu as pltpu
from jax.sharding import PartitionSpec as P

RANK = 8
MESH = pl.DeviceIdType.MESH
F32 = jnp.float32
BF16 = jnp.bfloat16


def tile_of(size, most):
    return most if size % most == 0 else size


def partner(me, d, size):
    bit, other = 1, me
    while bit < size:
        if d & bit:
            other = other + bit - 2 * bit * lax.rem(lax.div(me, jnp.int32(bit)), 2)
        bit *= 2
    return other


def dot(a, b):
    return jnp.dot(a, b, preferred_element_type=F32)


def kernel(
    E,
    H,
    C,
    cap,
    tok_ref,
    ids_ref,
    wt_ref,
    slot_ref,
    gw_hbm,
    uw_hbm,
    dw_hbm,
    ad_hbm,
    au_hbm,
    out_ref,
    gw,
    uw,
    dw,
    ad,
    au,
    zsend,
    zrecv,
    xrows,
    xrank,
    rank_own,
    rank_out,
    act,
    pout,
    pin,
    yown,
    rbuf,
    ret,
    comb,
    w_sem,
    z_s,
    z_r,
    x_s,
    x_r,
    k_s,
    k_r,
    o_s,
    o_r,
    b_s,
    b_r,
):
    me_e = lax.axis_index("expert")
    me_h = lax.axis_index("hidden")
    T, Dsh = tok_ref.shape
    K = ids_ref.shape[0]
    U = slot_ref.shape[1]
    F = gw.shape[1]
    A = ad.shape[1]
    W = Dsh // C

    def piece(c):
        return pl.ds(c * W, W)

    loads = [
        pltpu.make_async_copy(src.at[0], dst, w_sem.at[i])
        for i, (src, dst) in enumerate(
            ((ad_hbm, ad), (gw_hbm, gw), (uw_hbm, uw), (au_hbm, au), (dw_hbm, dw))
        )
    ]
    for load in loads:
        load.start()

    barrier = pltpu.get_barrier_semaphore()
    for d in range(1, E):
        pl.semaphore_signal(
            barrier, inc=1, device_id={"expert": partner(me_e, d, E)}, device_id_type=MESH
        )
    for j in range(1, H):
        pl.semaphore_signal(
            barrier, inc=1, device_id={"hidden": lax.rem(me_h + j, H)}, device_id_type=MESH
        )

    def z_copy(d, c):
        part = pl.ds(c * W, W + (A if c == C - 1 else 0))
        return pltpu.make_async_remote_copy(
            src_ref=zsend.at[d, :, part],
            dst_ref=zrecv.at[d, :, part],
            send_sem=z_s.at[d, c],
            recv_sem=z_r.at[d, c],
            device_id={"expert": partner(me_e, d, E)},
            device_id_type=MESH,
        )

    def x_copy(d, j, c):
        return pltpu.make_async_remote_copy(
            src_ref=zrecv.at[d, :, piece(c)],
            dst_ref=xrows.at[j, d, :, piece(c)],
            send_sem=x_s.at[j, d, c],
            recv_sem=x_r.at[j, d, c],
            device_id={"hidden": lax.rem(me_h + j, H)},
            device_id_type=MESH,
        )

    def k_copy(d, j):
        return pltpu.make_async_remote_copy(
            src_ref=rank_out.at[d],
            dst_ref=xrank.at[j, d],
            send_sem=k_s.at[j, d],
            recv_sem=k_r.at[j, d],
            device_id={"hidden": lax.rem(me_h + j, H)},
            device_id_type=MESH,
        )

    def o_copy(d, j, c):
        return pltpu.make_async_remote_copy(
            src_ref=pout.at[j, d, :, piece(c)],
            dst_ref=pin.at[j, d, :, piece(c)],
            send_sem=o_s.at[j, d, c],
            recv_sem=o_r.at[j, d, c],
            device_id={"hidden": lax.rem(me_h + j, H)},
            device_id_type=MESH,
        )

    def b_copy(d, c):
        return pltpu.make_async_remote_copy(
            src_ref=rbuf.at[d, :, piece(c)],
            dst_ref=ret.at[d, :, piece(c)],
            send_sem=b_s.at[d, c],
            recv_sem=b_r.at[d, c],
            device_id={"expert": partner(me_e, d, E)},
            device_id_type=MESH,
        )

    R = max(E, 8)
    ids = ids_ref[...]
    wts = wt_ref[...]
    turn = lax.broadcasted_iota(jnp.int32, (R, T), 0)
    named = jnp.full((R, T), -1, jnp.int32)
    for d in range(E):
        named = jnp.where(turn == d, partner(me_e, d, E), named)
    chosen = jnp.zeros((R, T), F32)
    weight = jnp.zeros((R, T), F32)
    for k in range(K):
        hit = ids[k : k + 1, :] == named
        chosen += jnp.where(hit, 1.0, 0.0)
        weight += jnp.where(hit, wts[k : k + 1, :], 0.0)
    before = lax.broadcasted_iota(jnp.int32, (T, T), 0) < lax.broadcasted_iota(
        jnp.int32, (T, T), 1
    )
    place = dot(chosen.astype(BF16), jnp.where(before, 1.0, 0.0).astype(BF16))
    place = jnp.where(chosen > 0.0, place, -1.0)
    row_no = lax.broadcasted_iota(jnp.int32, (cap, T), 0).astype(F32)
    picks = [row_no == place[d : d + 1, :] for d in range(E)]
    select = jnp.concatenate([jnp.where(p, 1.0, 0.0) for p in picks], axis=0).astype(BF16)
    slots = slot_ref[...].astype(F32)
    slot_no = lax.broadcasted_iota(jnp.int32, slots.shape, 0)
    eye = lax.broadcasted_iota(jnp.int32, (U, U), 0) == lax.broadcasted_iota(
        jnp.int32, (U, U), 1
    )
    column_slot = (lax.broadcasted_iota(jnp.int32, (U, A), 1) // RANK).astype(F32)

    def mask_of(d):
        row = jnp.sum(
            jnp.where(slot_no == partner(me_e, d, E), slots, 0.0), axis=0, keepdims=True
        )
        column = jnp.sum(jnp.where(eye, row, 0.0), axis=1, keepdims=True)
        user = jnp.where(column == column_slot, 1.0, 0.0)
        tokens = jnp.broadcast_to(user[:, None, :], (U, T // U, A)).reshape(T, A)
        return dot(select[d * cap : (d + 1) * cap], tokens.astype(BF16)).astype(BF16)

    tok = tok_ref[...]
    picked = dot(select, tok).astype(BF16)
    for d in range(E):
        block = zrecv if d == 0 else zsend
        block[d, :, pl.ds(0, Dsh)] = picked[d * cap : (d + 1) * cap]
        block[d, :, pl.ds(Dsh, A)] = mask_of(d)

    pl.semaphore_wait(barrier, E + H - 2)
    for d in range(1, E):
        for c in range(C):
            z_copy(d, c).start()

    loads[0].wait()

    def forward(d):
        for c in range(C):
            if d:
                z_copy(d, c).wait_recv()
            for j in range(1, H):
                x_copy(d, j, c).start()
        mine = dot(zrecv[d, :, pl.ds(0, Dsh)], ad[...])
        mine = jnp.where(zrecv[d, :, pl.ds(Dsh, A)] > 0, mine, 0.0)
        rank_own[d] = mine
        rank_out[d] = mine.astype(BF16)
        for j in range(1, H):
            k_copy(d, j).start()

    forward(0)
    scaled = jnp.concatenate(
        [jnp.where(p, weight[d : d + 1, :], 0.0) for d, p in enumerate(picks)], axis=0
    ).T
    high = scaled.astype(BF16)
    comb[pl.ds(0, T), :] = high
    comb[pl.ds(T, T), :] = (scaled - high.astype(F32)).astype(BF16)
    for load in loads[1:]:
        load.wait()

    tf = tile_of(F, 256)
    tn = tile_of(W, 512)

    def compute(d):
        for j in range(1, H):
            for c in range(C):
                x_copy(d, j, c).wait_recv()
            k_copy(d, j).wait_recv()
        rank = rank_own[d]
        for j in range(1, H):
            rank += xrank[j, d].astype(F32)
        rank = rank.astype(BF16)

        for c in range(F // tf):
            columns = pl.ds(c * tf, tf)
            up = dot(rank, au[:, columns])
            gate = jnp.zeros_like(up)
            for j in range(H):
                rows = pl.ds(pl.multiple_of(lax.rem(me_h - j + H, H) * Dsh, Dsh), Dsh)
                left = zrecv[d, :, pl.ds(0, Dsh)] if j == 0 else xrows[j, d]
                gate += dot(left, gw[rows, columns])
                up += dot(left, uw[rows, columns])
            act[:, columns] = (gate / (1.0 + jnp.exp(-gate)) * up).astype(BF16)

        def down(j, c):
            start = lax.rem(me_h + j, H) * Dsh + c * W

            @pl.loop(0, W // tn)
            def _(n):
                columns = pl.ds(pl.multiple_of(start + n * tn, tn), tn)
                part = dot(act[...], dw[:, columns]).astype(BF16)
                here = pl.ds(pl.multiple_of(c * W + n * tn, tn), tn)
                if j == 0:
                    yown[d, :, here] = part
                else:
                    pout[j, d, :, here] = part

            if j:
                o_copy(d, j, c).start()

        for j in range(1, H):
            for c in range(C):
                down(j, c)
        for c in range(C):
            down(0, c)

    def give_back(d):
        for c in range(C):
            total = yown[d, :, piece(c)].astype(F32)
            for j in range(1, H):
                o_copy(d, j, c).wait_recv()
                total += pin[j, d, :, piece(c)].astype(F32)
            if d:
                rbuf[d, :, piece(c)] = total.astype(BF16)
                b_copy(d, c).start()
            else:
                ret[0, :, piece(c)] = total.astype(BF16)

    for d in range(1, E):
        forward(d)
        if d > 1:
            compute(d - 1)
        if d > 2:
            give_back(d - 2)
    compute(E - 1)
    if E > 2:
        give_back(E - 2)
    compute(0)
    give_back(E - 1)
    give_back(0)

    for c in range(C):
        for d in range(1, E):
            b_copy(d, c).wait_recv()
        both = dot(comb[...], ret[:, :, piece(c)].reshape(E * cap, W))
        out_ref[:, piece(c)] = (both[:T] + both[T:]).astype(BF16)

    for d in range(E):
        for j in range(1, H):
            for c in range(C):
                x_copy(d, j, c).wait_send()
                o_copy(d, j, c).wait_send()
            k_copy(d, j).wait_send()
        if d:
            for c in range(C):
                z_copy(d, c).wait_send()
                b_copy(d, c).wait_send()


def local(
    tokens,
    route_ids,
    route_weight,
    user_slot,
    gate_weight,
    up_weight,
    down_weight,
    adapter_down,
    adapter_up,
):
    E = lax.axis_size("expert")
    H = lax.axis_size("hidden")
    T, K = route_ids.shape
    cap = T * K * 3 // (2 * E)
    Dsh = tokens.shape[1]
    D = gate_weight.shape[1]
    F = gate_weight.shape[2]
    A = adapter_down.shape[2]
    vmem = pl.BlockSpec(memory_space=pltpu.VMEM)
    hbm = pl.BlockSpec(memory_space=pl.ANY)
    dma = pltpu.SemaphoreType.DMA
    rows = E * cap
    C = 2 if Dsh % 1024 == 0 else 1
    flops = 2 * rows * (3 * D * F + Dsh * A + A * F)
    return pl.pallas_call(
        functools.partial(kernel, E, H, C, cap),
        out_shape=jax.ShapeDtypeStruct((T, Dsh), BF16),
        in_specs=[vmem] * 4 + [hbm] * 5,
        out_specs=vmem,
        scratch_shapes=[
            pltpu.VMEM((D, F), BF16),
            pltpu.VMEM((D, F), BF16),
            pltpu.VMEM((F, D), BF16),
            pltpu.VMEM((Dsh, A), BF16),
            pltpu.VMEM((A, F), BF16),
            pltpu.VMEM((E, cap, Dsh + A), BF16),
            pltpu.VMEM((E, cap, Dsh + A), BF16),
            pltpu.VMEM((H, E, cap, Dsh), BF16),
            pltpu.VMEM((H, E, cap, A), BF16),
            pltpu.VMEM((E, cap, A), F32),
            pltpu.VMEM((E, cap, A), BF16),
            pltpu.VMEM((cap, F), BF16),
            pltpu.VMEM((H, E, cap, Dsh), BF16),
            pltpu.VMEM((H, E, cap, Dsh), BF16),
            pltpu.VMEM((E, cap, Dsh), BF16),
            pltpu.VMEM((E, cap, Dsh), BF16),
            pltpu.VMEM((E, cap, Dsh), BF16),
            pltpu.VMEM((2 * T, rows), BF16),
            dma((5,)),
            dma((E, C)),
            dma((E, C)),
            dma((H, E, C)),
            dma((H, E, C)),
            dma((H, E)),
            dma((H, E)),
            dma((H, E, C)),
            dma((H, E, C)),
            dma((E, C)),
            dma((E, C)),
        ],
        compiler_params=pltpu.CompilerParams(
            collective_id=0, has_side_effects=True, vmem_limit_bytes=56 * 1024 * 1024
        ),
        cost_estimate=pl.CostEstimate(
            flops=flops, bytes_accessed=6 * D * F, transcendentals=rows * F
        ),
    )(
        tokens,
        route_ids.T,
        route_weight.T,
        user_slot.T,
        gate_weight,
        up_weight,
        down_weight,
        adapter_down,
        adapter_up,
    )


def solution(mesh):
    in_specs = (
        P(("parts", "expert", "rep"), "hidden"),
        P(("parts", "expert", "rep"), None),
        P(("parts", "expert", "rep"), None),
        P(("parts", "expert", "rep"), None),
        P("expert", None, "hidden"),
        P("expert", None, "hidden"),
        P("expert", "hidden", None),
        P("expert", "hidden", None),
        P("expert", None, "hidden"),
    )
    out_specs = P(("parts", "expert", "rep"), "hidden")
    return jax.shard_map(local, mesh=mesh, in_specs=in_specs, out_specs=out_specs, check_vma=False)
```
